128 devices in a mesh: slab: 2 (over z_lo), trow: 4 (over y), tcol: 16 (over x, z_hi, core).
Axes of the slice: x: 4, y: 4, z: 4 (z_hi: 2, z_lo: 2; z = z_hi * 2 + z_lo), core: 2. Of those that a mesh axis runs over, the one named last changes fastest.
Arguments:
- design: bfloat16 [4096, 16384], P('slab', ('tcol', 'trow')), may hold values from -6 to 6
- targets: float32 [4096], P('slab'), may hold values from -8 to 8
- coeffs: bfloat16 [16384], P(('tcol', 'trow')), may hold values from -0.046875 to 0.046875
- threshold: float32 [1], replicated, may hold values from 0.5 to 2
- damping: float32 [1], replicated, may hold values from 0.1 to 1
Outputs:
- hessian: float32 [16, 4, 256, 16384], P('slab', 'trow', None, 'tcol')
- gradient: float32 [16384], P(('tcol', 'trow'))
The draws below stay inside these ranges and needn't reach their ends.
All inputs are finite; a program needn't handle non-finite values.
Results may differ from the reference program's by a relative error of at most 0.0012.
Values may be sent and summed in bfloat16 or wider, within the bound.
No kernel may reach another device: no remote copies, remote signals or barrier semaphores. Data moves between devices by JAX's collectives and lax.ppermute only.
A program may use at most 192 MiB of HBM per device.

```python
import math
import jax
import jax.numpy as jnp
from jax import lax

P_SIZE = 16384
SAMPLES = 4096
N_TROW = 4
N_TCOL = 16


def steps_of(key, dims, pieces, low, high):
    level = 1.0
    for axis_at, parts in pieces:
        steps = jax.random.uniform(jax.random.fold_in(jax.random.fold_in(key, 6), axis_at), (parts,), jnp.float32, low / len(pieces), high / len(pieces))
        level = level * jnp.repeat(jnp.exp(steps), dims[axis_at] // parts).reshape((-1,) + (1,) * (len(dims) - 1 - axis_at))
    return level


def noise(rng, extent, width, limit, split=(), held_as=jnp.bfloat16):
    result = width * jax.random.normal(rng, extent, jnp.float32)
    if split:
        result = result * steps_of(rng, extent, split, -0.22, 0.18)
    return jnp.clip(result, -limit, limit).astype(held_as)


def setup_inputs(seed: int = 0) -> dict:
    arg_keys = jax.random.split(jax.random.key(seed), 6)
    return {
        "design": noise(arg_keys[0], (SAMPLES, P_SIZE), 1.0, 6.0, ((0, 2), (1, 64))),
        "targets": noise(arg_keys[1], (SAMPLES,), 1.5, 8.0, ((0, 2),), jnp.float32),
        "coeffs": noise(arg_keys[2], (P_SIZE,), P_SIZE ** -0.5, 0.046875, ((0, 64),)),
        "threshold": jnp.clip(jnp.exp(jax.random.uniform(arg_keys[3], (1,), jnp.float32, math.log(0.5), math.log(2.0))), 0.5, 2.0),
        "damping": jnp.clip(jnp.exp(jax.random.uniform(arg_keys[4], (1,), jnp.float32, math.log(0.1), math.log(1.0))), 0.1, 1.0),
    }


def reference(design, targets, coeffs, threshold, damping):
    predicted = jnp.dot(design, coeffs, preferred_element_type=jnp.float32)
    residual = targets - predicted
    cutoff = threshold[0]
    weight = cutoff / jnp.maximum(jnp.abs(residual), cutoff)
    influence = weight * residual
    dense = design.astype(jnp.float32)
    samples = design.shape[0]
    gradient = -jnp.dot(influence, dense, precision=lax.Precision.HIGHEST) / samples
    weighted = lax.optimization_barrier((dense * weight[:, None]).astype(jnp.bfloat16)).astype(jnp.float32)
    gram = jnp.dot(dense.T, weighted, precision=lax.Precision.HIGHEST) / samples
    diag_index = jnp.arange(P_SIZE, dtype=jnp.int32)
    gram = gram.at[diag_index, diag_index].add(damping[0])
    hessian = gram.reshape(N_TCOL, N_TROW, P_SIZE // (N_TROW * N_TCOL), P_SIZE)
    return hessian, gradient
```

```python
import functools

import jax
import jax.numpy as jnp
from jax import lax
from jax.experimental import pallas as pl
from jax.experimental.pallas import tpu as pltpu
from jax.sharding import PartitionSpec as P

AXES = ("slab", "trow", "tcol")
N_X, N_Y, N_Z, N_CORE = 4, 4, 4, 2


def index_of(x, y, z, core):
    return ((z % 2) * N_Y + y) * 16 + x * 4 + (z // 2) * 2 + core


def is_native(x, z):
    return (x // 2) == (z % 2)


def pairs(x=0, y=0, z=0, core=0, senders=None):
    found = []
    for cx in range(N_X):
        for cy in range(N_Y):
            for cz in range(N_Z):
                if senders is not None and not senders(cx, cz):
                    continue
                for ck in range(N_CORE):
                    found.append((index_of(cx, cy, cz, ck), index_of(cx ^ x, cy ^ y, cz ^ z, ck ^ core)))
    return found


def move(value, **where):
    return lax.ppermute(value, AXES, pairs(**where))


def weigh_kernel(blocks_ref, weight_ref, *refs):
    *shard_refs, out_ref = refs
    width = shard_refs[0].shape[1]
    lanes = weight_ref.shape[1]
    weight = weight_ref[...]
    for m, shard_ref in enumerate(shard_refs):
        base = blocks_ref[m] * width
        for part in range(width // lanes):
            scaled = shard_ref[:, part * lanes:(part + 1) * lanes].astype(jnp.float32) * weight
            at = pl.multiple_of(base + part * lanes, lanes)
            out_ref[:, pl.ds(at, lanes)] = scaled.astype(jnp.bfloat16)


def weigh(blocks, weight, shards):
    rows, width = shards[0].shape
    spread = jnp.broadcast_to(weight[:, None], (rows, 128))
    vmem = pl.BlockSpec(memory_space=pltpu.VMEM)
    return pl.pallas_call(
        weigh_kernel,
        out_shape=jax.ShapeDtypeStruct((rows, width * len(shards)), jnp.bfloat16),
        in_specs=[pl.BlockSpec(memory_space=pltpu.SMEM)] + [vmem] * (1 + len(shards)),
        out_specs=vmem,
        compiler_params=pltpu.CompilerParams(vmem_limit_bytes=40 * 2**20),
        cost_estimate=pl.CostEstimate(flops=rows * width * 4, bytes_accessed=rows * width * 18, transcendentals=0),
        name="weigh",
    )(blocks, spread, *shards)


def gram_kernel(meta_ref, damping_ref, lhs_ref, own_ref, other_ref, *refs, samples):
    out_ref = refs[-1]
    step = pl.program_id(0)
    steps = pl.num_programs(0)
    contract = (((0,), (0,)), ((), ()))
    total = lax.dot_general(lhs_ref[0, 0], own_ref[...], contract, preferred_element_type=jnp.float32)
    total += lax.dot_general(lhs_ref[0, 1], other_ref[...], contract, preferred_element_type=jnp.float32)
    out_ref[0] = total * (1.0 / samples)

    @pl.when(meta_ref[steps + step] == 1)
    def _():
        height = out_ref.shape[1]
        at = pl.multiple_of(meta_ref[2 * steps] * height, height)
        eye = (lax.broadcasted_iota(jnp.int32, (height, height), 0)
               == lax.broadcasted_iota(jnp.int32, (height, height), 1))
        out_ref[0, :, pl.ds(at, height)] += jnp.where(eye, damping_ref[0], 0.0)


def gram_blocks(lhs, own, other, damping, tiles, diagonal, row, samples, into=None):
    count, _, rows, height = lhs.shape
    width = own.shape[1]
    meta = jnp.concatenate([tiles, diagonal, row[None]]).astype(jnp.int32)
    whole = pl.BlockSpec((rows, width), lambda i, meta: (0, 0), pipeline_mode=pl.Buffered(1))
    in_specs = [
        pl.BlockSpec(memory_space=pltpu.SMEM),
        pl.BlockSpec((1, 2, rows, height), lambda i, meta: (i, 0, 0, 0)),
        whole,
        whole,
    ]
    operands = [meta, damping, lhs, own, other]
    aliases = {}
    if into is not None:
        in_specs.append(pl.BlockSpec(memory_space=pl.ANY))
        operands.append(into)
        aliases = {5: 0}
    flops = 2 * count * 2 * rows * height * width
    moved = count * (2 * rows * height * 2 + height * width * 4) + 4 * rows * width
    return pl.pallas_call(
        functools.partial(gram_kernel, samples=samples),
        out_shape=jax.ShapeDtypeStruct((8, height, width), jnp.float32),
        grid_spec=pltpu.PrefetchScalarGridSpec(
            num_scalar_prefetch=1,
            grid=(count,),
            in_specs=in_specs,
            out_specs=pl.BlockSpec((1, height, width), lambda i, meta: (meta[i], 0, 0)),
        ),
        input_output_aliases=aliases,
        compiler_params=pltpu.CompilerParams(vmem_limit_bytes=48 * 2**20),
        cost_estimate=pl.CostEstimate(flops=flops, bytes_accessed=moved, transcendentals=0),
        name="gram",
    )(*operands)


def local(design, targets, coeffs, threshold, damping):
    rows, width = design.shape
    samples = rows * lax.axis_size("slab")
    slab, row, col = lax.axis_index("slab"), lax.axis_index("trow"), lax.axis_index("tcol")
    x, zh, core = col // 4, (col // 2) % 2, col % 2
    native = (x // 2) == slab

    def pick(if_native, if_far):
        return jnp.where(native, if_native, if_far)

    columns = lax.all_gather(design, "trow", axis=1, tiled=True)

    from_zp = move(design, z=1)
    from_zo = move(design, z=3)
    from_xp = move(design, x=1, senders=is_native)
    from_xo = move(design, x=3)

    partial_value = jnp.dot(design, coeffs, preferred_element_type=jnp.float32).reshape(rows // 128, 128)
    for where in ({"core": 1}, {"x": 1}, {"y": 1}, {"x": 2}, {"y": 2}, {"z": 2}):
        partial_value = partial_value + move(partial_value, **where)
    residual = targets - partial_value.reshape(rows)
    residual_other = move(residual.reshape(rows // 128, 128), z=1).reshape(rows)
    cutoff = threshold[0]
    weight = cutoff / jnp.maximum(jnp.abs(residual), cutoff)
    weight_other = cutoff / jnp.maximum(jnp.abs(residual_other), cutoff)
    influence = weight * residual
    local_grad = jnp.dot(influence, design.astype(jnp.float32), precision=lax.Precision.HIGHEST)
    gradient = -(local_grad + move(local_grad, z=1)) / samples

    other_y1 = move(from_zp, y=1)
    other_y3 = move(from_zp, y=3)
    other_y2 = move(from_zp, y=2)

    second_xp = move(pick(from_zp, from_xo), x=1)
    second_zo = move(pick(from_xo, from_zp), z=3)
    second_zp = move(from_xo, z=1, senders=is_native)
    third_xp = move(pick(second_zo, second_zp), x=1)
    third_xo = move(second_zo, x=3, senders=is_native)
    fourth_xp = move(pick(from_zo, second_zo), x=1)
    fourth_xo = move(third_xp, x=3, senders=is_native)

    first_part = jnp.stack([
        jnp.stack([pick(design, from_xo), pick(from_zp, second_zp)]),
        jnp.stack([pick(second_zo, third_xo), pick(from_zo, second_zo)]),
        jnp.stack([pick(from_xp, second_xp), pick(second_xp, third_xp)]),
    ])
    last_part = jnp.stack([pick(third_xp, fourth_xo), fourth_xp])[None]
    first_sibling = move(first_part, core=1)
    last_sibling = move(last_part, core=1)

    order = jnp.arange(4, dtype=jnp.int32)
    own_weighted = (columns.astype(jnp.float32) * weight[:, None]).astype(jnp.bfloat16)
    other_weighted = weigh(row ^ order, weight_other, [from_zp, other_y1, other_y2, other_y3])

    column_a = pick(x, x ^ 3)
    column_b = column_a ^ 1

    def tile(column, half, core_at):
        return (column * 4 + half * 2 + core_at) - 8 * slab

    def fill(lhs, columns_halves, core_at, into):
        tiles = jnp.stack([tile(c, h, core_at) for c, h in columns_halves])
        diagonal = (tiles + 8 * slab == col).astype(jnp.int32)
        return gram_blocks(lhs, own_weighted, other_weighted, damping, tiles, diagonal, row, samples, into)

    first_at = [(column_a, zh), (column_a, 1 - zh), (column_b, zh)]
    last_at = [(column_b, 1 - zh)]
    result = fill(first_part, first_at, core, None)
    result = fill(first_sibling, first_at, 1 - core, result)
    result = fill(last_part, last_at, core, result)
    result = fill(last_sibling, last_at, 1 - core, result)
    hessian = result.reshape(8, 1, width, own_weighted.shape[1])
    return (hessian, gradient)


def solution(mesh):
    in_specs = (P("slab", ("tcol", "trow")), P("slab"), P(("tcol", "trow")), P(), P())
    out_specs = (P("slab", "trow", None, "tcol"), P(("tcol", "trow")))
    return jax.shard_map(local, mesh=mesh, in_specs=in_specs, out_specs=out_specs, check_vma=False)
```

```python
import functools

import jax
import jax.numpy as jnp
from jax import lax
from jax.experimental import pallas as pl
from jax.experimental.pallas import tpu as pltpu
from jax.sharding import PartitionSpec as P

AXES = ("slab", "trow", "tcol")
N_X, N_Y, N_Z, N_CORE = 4, 4, 4, 2


def index_of(x, y, z, core):
    return ((z % 2) * N_Y + y) * 16 + x * 4 + (z // 2) * 2 + core


def is_native(x, z):
    return (x // 2) == (z % 2)


def pairs(route):
    found = []
    for x in range(N_X):
        for y in range(N_Y):
            for z in range(N_Z):
                step = route(x, z)
                if step is None:
                    continue
                dx, dy, dz, dcore = step
                for core in range(N_CORE):
                    target = index_of(x ^ dx, y ^ dy, z ^ dz, core ^ dcore)
                    found.append((index_of(x, y, z, core), target))
    return found


def move(value, x=0, y=0, z=0, core=0):
    return lax.ppermute(value, AXES, pairs(lambda cx, cz: (x, y, z, core)))


def move_by_role(value, native=None, far=None):
    return lax.ppermute(value, AXES, pairs(lambda cx, cz: native if is_native(cx, cz) else far))


def weigh_kernel(blocks_ref, spread_ref, *refs, places):
    *shard_refs, out_ref = refs
    lanes = spread_ref.shape[1]
    for m, shard_ref in zip(places, shard_refs):
        width = shard_ref.shape[1]
        for part in range(0, width, lanes):
            scaled = shard_ref[:, part:part + lanes].astype(jnp.float32) * spread_ref[...]
            at = pl.multiple_of(blocks_ref[m] * width + part, lanes)
            out_ref[:, pl.ds(at, lanes)] = scaled.astype(jnp.bfloat16)


def weigh(blocks, spread, shards, places):
    rows, width = shards[0].shape
    step = rows // 4

    def block(columns):
        return pl.BlockSpec((step, columns), lambda i, blocks: (i, 0))

    return pl.pallas_call(
        functools.partial(weigh_kernel, places=places),
        out_shape=jax.ShapeDtypeStruct((rows, width * N_Y), jnp.bfloat16),
        grid_spec=pltpu.PrefetchScalarGridSpec(
            num_scalar_prefetch=1,
            grid=(rows // step,),
            in_specs=[block(spread.shape[1])] + [block(width)] * len(shards),
            out_specs=block(width * N_Y),
        ),
        compiler_params=pltpu.CompilerParams(vmem_limit_bytes=60 * 2**20),
        cost_estimate=pl.CostEstimate(flops=0, bytes_accessed=0, transcendentals=0),
        name="weigh",
    )(blocks, spread, *shards)


N_TILES = 4
TILE_AT, DIAGONAL_AT, OWN_AT, OTHER_AT, ROW_AT, BLOCK_AT = 0, 4, 8, 12, 16, 17
FIRST_NEEDS, LATER_NEEDS = (1, 3), ((2, 6), (7, 5), (4,))


def gram_kernel(meta_ref, damping_ref, own_hbm, shards_hbm, *refs, samples, fresh):
    if fresh:
        before_hbm, spread_hbm, column_hbm = refs[:3]
        out_ref, other_hbm, weighted, slots, weighted_sems, slot_sems, column, spread, column_sems = refs[3:]
    else:
        before_hbm = refs[0]
        out_ref, weighted, slots, weighted_sems, slot_sems = refs[2:]
    step = pl.program_id(0)
    contract = (((0,), (0,)), ((), ()))
    scale = 1.0 / samples

    def slot_copy(n):
        return pltpu.make_async_copy(shards_hbm.at[n], slots.at[n], slot_sems.at[n])

    def product(n, at):
        return lax.dot_general(
            slots[meta_ref[at + step]], weighted[n], contract, preferred_element_type=jnp.float32)

    own_copy = pltpu.make_async_copy(own_hbm, weighted.at[0], weighted_sems.at[0])
    other_copy = pltpu.make_async_copy(before_hbm, weighted.at[1], weighted_sems.at[1])
    if fresh:
        column_copies = (
            pltpu.make_async_copy(column_hbm, column, column_sems.at[0]),
            pltpu.make_async_copy(spread_hbm, spread, column_sems.at[1]))
        hand_on = pltpu.make_async_copy(weighted.at[1], other_hbm, weighted_sems.at[1])

    def scale_column():
        rows, width = column.shape
        lanes = spread.shape[1]
        chunk = 512

        @pl.loop(0, rows // chunk)
        def _(i):
            at_rows = pl.ds(pl.multiple_of(i * chunk, chunk), chunk)
            weight = spread[at_rows, :]
            for part in range(0, width, lanes):
                scaled = column[at_rows, part:part + lanes].astype(jnp.float32) * weight
                at = pl.multiple_of(meta_ref[BLOCK_AT] * width + part, lanes)
                weighted[1, at_rows, pl.ds(at, lanes)] = scaled.astype(jnp.bfloat16)

    @pl.when(step == 0)
    def _():
        own_copy.start()
        slot_copy(0).start()
        if fresh:
            for copy in column_copies:
                copy.start()
        other_copy.start()
        for n in FIRST_NEEDS:
            slot_copy(n).start()
        own_copy.wait()
        slot_copy(0).wait()
        out_ref[0] = product(0, OWN_AT)
        other_copy.wait()
        if fresh:
            for copy in column_copies:
                copy.wait()
            scale_column()
            hand_on.start()
        for n in FIRST_NEEDS:
            slot_copy(n).wait()
        for needed in LATER_NEEDS:
            for n in needed:
                slot_copy(n).start()
        out_ref[0] = (out_ref[0] + product(1, OTHER_AT)) * scale

    for at, needed in enumerate(LATER_NEEDS):
        @pl.when(step == at + 1)
        def _(needed=needed):
            for n in needed:
                slot_copy(n).wait()

    @pl.when(step > 0)
    def _():
        out_ref[0] = (product(0, OWN_AT) + product(1, OTHER_AT)) * scale

    @pl.when(meta_ref[DIAGONAL_AT + step] == 1)
    def _():
        height = out_ref.shape[1]
        at = pl.multiple_of(meta_ref[ROW_AT] * height, height)
        eye = (lax.broadcasted_iota(jnp.int32, (height, height), 0)
               == lax.broadcasted_iota(jnp.int32, (height, height), 1))
        out_ref[0, :, pl.ds(at, height)] += jnp.where(eye, damping_ref[0], 0.0)

    if fresh:
        @pl.when(step == N_TILES - 1)
        def _():
            hand_on.wait()


def gram_blocks(meta, damping, own, other, shards, samples, spread=None, column=None, into=None):
    _, rows, height = shards.shape
    width = own.shape[1]
    fresh = into is None
    hbm = pl.BlockSpec(memory_space=pl.ANY)
    arrays = [meta, damping, own, shards] + ([other, spread, column] if fresh else [other, into])
    result = jax.ShapeDtypeStruct((2 * N_TILES, height, width), jnp.float32)
    block = pl.BlockSpec((1, height, width), lambda i, meta: (meta[i], 0, 0))
    scratch = [
        pltpu.VMEM((2, rows, width), jnp.bfloat16),
        pltpu.VMEM((8, rows, height), jnp.bfloat16),
        pltpu.SemaphoreType.DMA((2,)),
        pltpu.SemaphoreType.DMA((8,)),
    ]
    if fresh:
        scratch += [
            pltpu.VMEM((rows, height), jnp.bfloat16),
            pltpu.VMEM(spread.shape, jnp.float32),
            pltpu.SemaphoreType.DMA((2,)),
        ]
    flops = N_TILES * 2 * 2 * rows * height * width
    moved = 8 * rows * height * 2 + N_TILES * height * width * 4 + 4 * rows * width
    return pl.pallas_call(
        functools.partial(gram_kernel, samples=samples, fresh=fresh),
        out_shape=(result, jax.ShapeDtypeStruct(own.shape, own.dtype)) if fresh else result,
        grid_spec=pltpu.PrefetchScalarGridSpec(
            num_scalar_prefetch=1,
            grid=(N_TILES,),
            in_specs=[pl.BlockSpec(memory_space=pltpu.SMEM)] + [hbm] * (len(arrays) - 2),
            out_specs=(block, hbm) if fresh else block,
            scratch_shapes=scratch,
        ),
        input_output_aliases={} if fresh else {len(arrays) - 1: 0},
        compiler_params=pltpu.CompilerParams(vmem_limit_bytes=60 * 2**20),
        cost_estimate=pl.CostEstimate(flops=flops, bytes_accessed=moved, transcendentals=0),
        name="gram_first" if fresh else "gram",
    )(*arrays)


def local(design, targets, coeffs, threshold, damping):
    rows, width = design.shape
    samples = rows * lax.axis_size("slab")
    slab, row, col = lax.axis_index("slab"), lax.axis_index("trow"), lax.axis_index("tcol")
    x, zh, core = col // 4, (col // 2) % 2, col % 2
    native = (x // 2) == slab
    tie = lax.optimization_barrier

    def pick(if_native, if_far):
        return jnp.where(native, if_native, if_far)

    columns = lax.all_gather(design, "trow", axis=1, tiled=True)

    from_xo = move(design, x=3)
    first = (row == 0) & (col == 0)
    share = jnp.where(first, targets, 0.0) - jnp.dot(design, coeffs, preferred_element_type=jnp.float32)
    share = share.reshape(rows // 128, 128)
    share = share + move(share, z=2)
    design_z, share = tie((design, share))
    from_zp = move(design_z, z=1)
    from_zo = move(design_z, z=3)
    share = share + move(share, x=1)
    design_x, share = tie((design, share))
    from_xp = move(design_x, x=1)
    for where in ({"core": 1}, {"y": 1}, {"y": 2}, {"x": 3}):
        share = share + move(share, **where)
    from_zp, from_zo, from_xp, from_xo, share = tie((from_zp, from_zo, from_xp, from_xo, share))

    second_xp = move(from_xo, x=1)
    by_zo, by_zp, share_other = tie((pick(from_xo, from_zp), pick(from_xo, from_xp), move(share, z=1)))
    second_zo = move(by_zo, z=3)
    second_zp = move(by_zp, z=1)
    other_y1 = move(from_zp, y=1)
    other_y3 = move(from_zp, y=3)
    second_xp, from_xp = tie((second_xp, from_xp))
    by_z = pick(second_xp, from_xp)
    second_xp, second_zo, second_zp, by_z, share, from_zp_y = tie((second_xp, second_zo, second_zp, by_z, share, from_zp))

    third_xp = move(second_zo, x=1)
    third_xo = move_by_role(second_zo, native=(3, 0, 0, 0))
    third_z = move_by_role(by_z, native=(0, 0, 1, 0), far=(0, 0, 3, 0))
    by_z2, from_zp_y, other_y1, other_y3 = tie((second_xp, from_zp_y, other_y1, other_y3))
    third_z2 = move_by_role(by_z2, far=(0, 0, 2, 0))
    other_y2 = move(from_zp_y, y=2)

    cutoff = threshold[0]
    residual, residual_other = share.reshape(rows), share_other.reshape(rows)
    weight = cutoff / jnp.maximum(jnp.abs(residual), cutoff)
    weight_other = cutoff / jnp.maximum(jnp.abs(residual_other), cutoff)
    influence = weight * residual
    local_grad = jnp.dot(influence, design.astype(jnp.float32), precision=lax.Precision.HIGHEST)
    spread = jnp.broadcast_to(weight_other[:, None], (rows, 128))
    blocks = row ^ jnp.arange(N_Y, dtype=jnp.int32)
    columns, other_y1, other_y3 = tie((columns, other_y1, other_y3))
    own_weighted = (columns.astype(jnp.float32) * weight[:, None]).astype(jnp.bfloat16)
    other_weighted = weigh(blocks, spread, [from_zp, other_y1, other_y3], (0, 1, 3))
    third_z, own_weighted, other_weighted, spread, local_grad = tie(
        (third_z, own_weighted, other_weighted, spread, local_grad))
    here = jnp.stack([
        pick(design, from_xo), pick(from_zp, second_xp), second_zo, second_zp,
        third_xp, third_z, pick(from_zo, third_xo), pick(from_xp, third_z2)])
    here, other_y2 = tie((here, other_y2))

    sibling = move(here, core=1)

    column_a = pick(x, x ^ 3)
    column_b = column_a ^ 1
    own_slots = pick(jnp.array([0, 2, 7, 4]), jnp.array([0, 6, 1, 7]))
    other_slots = pick(jnp.array([1, 6, 3, 5]), jnp.array([3, 2, 5, 4]))

    def describe(core_at):
        places = ((column_a, zh), (column_a, 1 - zh), (column_b, zh), (column_b, 1 - zh))
        tiles = jnp.stack([column * 4 + at * 2 + core_at - 8 * slab for column, at in places])
        diagonal = tiles + 8 * slab == col
        return jnp.concatenate([tiles, diagonal, own_slots, other_slots, row[None], blocks[2:3]]).astype(jnp.int32)

    result, other_weighted = gram_blocks(
        describe(core), damping, own_weighted, other_weighted, here, samples, spread=spread, column=other_y2)
    result, local_grad = tie((result, local_grad))
    gradient = -(local_grad + move(local_grad, z=1)) / samples
    result = gram_blocks(
        describe(1 - core), damping, own_weighted, other_weighted, sibling, samples, into=result)
    hessian = result.reshape(2 * N_TILES, 1, width, columns.shape[1])
    return (hessian, gradient)


def solution(mesh):
    in_specs = (P("slab", ("tcol", "trow")), P("slab"), P(("tcol", "trow")), P(), P())
    out_specs = (P("slab", "trow", None, "tcol"), P(("tcol", "trow")))
    return jax.shard_map(local, mesh=mesh, in_specs=in_specs, out_specs=out_specs, check_vma=False)
```

```python
import functools

import jax
import jax.numpy as jnp
from jax import lax
from jax.experimental import pallas as pl
from jax.experimental.pallas import tpu as pltpu
from jax.sharding import PartitionSpec as P

AXES = ("slab", "trow", "tcol")
N_X, N_Y, N_Z, N_CORE = 4, 4, 4, 2


def index_of(x, y, z, core):
    return ((z % 2) * N_Y + y) * 16 + x * 4 + (z // 2) * 2 + core


def is_native(x, z):
    return (x // 2) == (z % 2)


def pairs(route):
    found = []
    for x in range(N_X):
        for y in range(N_Y):
            for z in range(N_Z):
                step = route(x, z)
                if step is None:
                    continue
                dx, dy, dz, dcore = step
                for core in range(N_CORE):
                    target = index_of(x ^ dx, y ^ dy, z ^ dz, core ^ dcore)
                    found.append((index_of(x, y, z, core), target))
    return found


def move(value, x=0, y=0, z=0, core=0):
    return lax.ppermute(value, AXES, pairs(lambda cx, cz: (x, y, z, core)))


def move_by_role(value, native=None, far=None):
    return lax.ppermute(value, AXES, pairs(lambda cx, cz: native if is_native(cx, cz) else far))


def weigh_kernel(blocks_ref, spread_ref, *refs, places):
    *shard_refs, out_ref = refs
    lanes = spread_ref.shape[1]
    for m, shard_ref in zip(places, shard_refs):
        width = shard_ref.shape[1]
        for part in range(0, width, lanes):
            scaled = shard_ref[:, part:part + lanes].astype(jnp.float32) * spread_ref[...]
            at = pl.multiple_of(blocks_ref[m] * width + part, lanes)
            out_ref[:, pl.ds(at, lanes)] = scaled.astype(jnp.bfloat16)


def weigh(blocks, spread, shards, places):
    rows, width = shards[0].shape
    step = rows // 4

    def block(columns):
        return pl.BlockSpec((step, columns), lambda i, blocks: (i, 0))

    return pl.pallas_call(
        functools.partial(weigh_kernel, places=places),
        out_shape=jax.ShapeDtypeStruct((rows, width * N_Y), jnp.bfloat16),
        grid_spec=pltpu.PrefetchScalarGridSpec(
            num_scalar_prefetch=1,
            grid=(rows // step,),
            in_specs=[block(spread.shape[1])] + [block(width)] * len(shards),
            out_specs=block(width * N_Y),
        ),
        compiler_params=pltpu.CompilerParams(vmem_limit_bytes=60 * 2**20),
        cost_estimate=pl.CostEstimate(flops=0, bytes_accessed=0, transcendentals=0),
        name="weigh",
    )(blocks, spread, *shards)


N_TILES = 4
TILE_AT, DIAGONAL_AT, OWN_AT, OTHER_AT, ROW_AT, BLOCK_AT = 0, 4, 8, 12, 16, 17
FIRST_NEEDS, LATER_NEEDS = (1, 3), ((2, 6), (7, 5), (4,))
N_CHUNKS = 4
AHEAD = 8


def gram_kernel(meta_ref, damping_ref, own_hbm, stack_hbm, *refs, samples, fresh):
    shards_hbm = [stack_hbm.at[n] for n in range(4)] + list(refs[:4])
    refs = refs[4:]
    if fresh:
        before_hbm, spread_hbm, column_hbm = refs[:3]
        out_ref, other_hbm, weighted, slots, weighted_sems, slot_sems, column, spread, column_sems = refs[3:]
    else:
        before_hbm = refs[0]
        out_ref, weighted, slots, weighted_sems, slot_sems = refs[2:]
    step = pl.program_id(0)
    contract = (((0,), (0,)), ((), ()))
    scale = 1.0 / samples
    chunk = weighted.shape[1] // N_CHUNKS

    def slot_copy(n):
        return pltpu.make_async_copy(shards_hbm[n], slots.at[n], slot_sems.at[n])

    def product(n, at):
        return lax.dot_general(
            slots[meta_ref[at + step]], weighted[n], contract, preferred_element_type=jnp.float32)

    def rows_at(j):
        return pl.ds(j * chunk, chunk)

    def weighted_copy(n, j):
        source = (own_hbm, before_hbm)[n]
        return pltpu.make_async_copy(source.at[rows_at(j)], weighted.at[n, rows_at(j)], weighted_sems.at[n, j])

    def part(n, at, j):
        return lax.dot_general(
            slots[meta_ref[at], rows_at(j)], weighted[n, rows_at(j)], contract, preferred_element_type=jnp.float32)

    if fresh:
        column_copies = (
            pltpu.make_async_copy(column_hbm, column, column_sems.at[0]),
            pltpu.make_async_copy(spread_hbm, spread, column_sems.at[1]))
        hand_on = pltpu.make_async_copy(weighted.at[1], other_hbm, column_sems.at[2])

    def scale_column(j):
        width, lanes = column.shape[1], spread.shape[1]
        weight = spread[rows_at(j), :]
        for first in range(0, width, lanes):
            scaled = column[rows_at(j), first:first + lanes].astype(jnp.float32) * weight
            at = pl.multiple_of(meta_ref[BLOCK_AT] * width + first, lanes)
            weighted[1, rows_at(j), pl.ds(at, lanes)] = scaled.astype(jnp.bfloat16)

    @pl.when(step == 0)
    def _():
        queue = [slot_copy(0)] + [weighted_copy(0, j) for j in range(N_CHUNKS)]
        queue += [slot_copy(n) for n in FIRST_NEEDS]
        if fresh:
            queue += column_copies
        queue += [weighted_copy(1, j) for j in range(N_CHUNKS)]
        later = [slot_copy(n) for needed in LATER_NEEDS for n in needed]
        todo = queue + later
        for copy in todo[:AHEAD]:
            copy.start()
        waited = 0

        def wait(count):
            nonlocal waited
            for n in range(waited, waited + count):
                todo[n].wait()
                if n + AHEAD < len(todo):
                    todo[n + AHEAD].start()
            waited += count

        wait(1)
        for j in range(N_CHUNKS):
            wait(1)
            if j == 0:
                out_ref[0] = part(0, OWN_AT, j)
            else:
                out_ref[0] += part(0, OWN_AT, j)
        wait(len(FIRST_NEEDS) + (len(column_copies) if fresh else 0))
        for j in range(N_CHUNKS):
            wait(1)
            if fresh:
                scale_column(j)
            if j < N_CHUNKS - 1:
                out_ref[0] += part(1, OTHER_AT, j)
            else:
                out_ref[0] = (out_ref[0] + part(1, OTHER_AT, j)) * scale
        for copy in todo[waited + AHEAD:]:
            copy.start()
        if fresh:
            hand_on.start()

    for at, needed in enumerate(LATER_NEEDS):
        @pl.when(step == at + 1)
        def _(needed=needed):
            for n in needed:
                slot_copy(n).wait()

    @pl.when(step > 0)
    def _():
        out_ref[0] = (product(0, OWN_AT) + product(1, OTHER_AT)) * scale

    @pl.when(meta_ref[DIAGONAL_AT + step] == 1)
    def _():
        height = out_ref.shape[1]
        at = pl.multiple_of(meta_ref[ROW_AT] * height, height)
        eye = (lax.broadcasted_iota(jnp.int32, (height, height), 0)
               == lax.broadcasted_iota(jnp.int32, (height, height), 1))
        out_ref[0, :, pl.ds(at, height)] += jnp.where(eye, damping_ref[0], 0.0)

    if fresh:
        @pl.when(step == N_TILES - 1)
        def _():
            hand_on.wait()


def gram_blocks(meta, damping, own, other, shards, samples, spread=None, column=None, into=None):
    rows, height = shards[1].shape
    width = own.shape[1]
    fresh = into is None
    hbm = pl.BlockSpec(memory_space=pl.ANY)
    arrays = [meta, damping, own, *shards] + ([other, spread, column] if fresh else [other, into])
    result = jax.ShapeDtypeStruct((2 * N_TILES, height, width), jnp.float32)
    block = pl.BlockSpec((1, height, width), lambda i, meta: (meta[i], 0, 0))
    scratch = [
        pltpu.VMEM((2, rows, width), jnp.bfloat16),
        pltpu.VMEM((8, rows, height), jnp.bfloat16),
        pltpu.SemaphoreType.DMA((2, N_CHUNKS)),
        pltpu.SemaphoreType.DMA((8,)),
    ]
    if fresh:
        scratch += [
            pltpu.VMEM((rows, height), jnp.bfloat16),
            pltpu.VMEM(spread.shape, jnp.float32),
            pltpu.SemaphoreType.DMA((3,)),
        ]
    flops = N_TILES * 2 * 2 * rows * height * width
    moved = 8 * rows * height * 2 + N_TILES * height * width * 4 + 4 * rows * width
    return pl.pallas_call(
        functools.partial(gram_kernel, samples=samples, fresh=fresh),
        out_shape=(result, jax.ShapeDtypeStruct(own.shape, own.dtype)) if fresh else result,
        grid_spec=pltpu.PrefetchScalarGridSpec(
            num_scalar_prefetch=1,
            grid=(N_TILES,),
            in_specs=[pl.BlockSpec(memory_space=pltpu.SMEM)] + [hbm] * (len(arrays) - 2),
            out_specs=(block, hbm) if fresh else block,
            scratch_shapes=scratch,
        ),
        input_output_aliases={} if fresh else {len(arrays) - 1: 0},
        compiler_params=pltpu.CompilerParams(vmem_limit_bytes=60 * 2**20),
        cost_estimate=pl.CostEstimate(flops=flops, bytes_accessed=moved, transcendentals=0),
        name="gram_first" if fresh else "gram",
    )(*arrays)


def local(design, targets, coeffs, threshold, damping):
    rows, width = design.shape
    samples = rows * lax.axis_size("slab")
    slab, row, col = lax.axis_index("slab"), lax.axis_index("trow"), lax.axis_index("tcol")
    x, zh, core = col // 4, (col // 2) % 2, col % 2
    native = (x // 2) == slab
    tie = lax.optimization_barrier

    def pick(if_native, if_far):
        return jnp.where(native, if_native, if_far)

    first = (row == 0) & (col == 0)
    share = jnp.where(first, targets, 0.0) - jnp.dot(design, coeffs, preferred_element_type=jnp.float32)
    share = share.reshape(rows // 128, 128)
    share = share + move(share, z=2)
    design_z, share = tie((design, share))
    from_zp = move(design_z, z=1)
    from_zo = move(design_z, z=3)
    share = (share + move(share, x=1)) + (move(share, x=3) + move(share, x=2))
    design_x, share = tie((design, share))
    from_xo = move(design_x, x=3)
    from_xp = move(design_x, x=1)
    for where in ({"core": 1}, {"y": 1}, {"y": 2}):
        share = share + move(share, **where)
    design_y, share = tie((design, share))
    own_y1 = move(design_y, y=1)
    own_y3 = move(design_y, y=3)
    from_zp, from_zo, from_xp, from_xo, share = tie((from_zp, from_zo, from_xp, from_xo, share))

    second_xp = move(from_xo, x=1)
    by_zo, by_zp, shares = tie(
        (pick(from_xo, from_zp), pick(from_xo, from_xp), jnp.stack([share, move(share, z=1)])))
    second_zo = move(by_zo, z=3)
    second_zp = move(by_zp, z=1)
    by_y1, own_y1 = tie((from_zp, own_y1))
    other_y1 = move(by_y1, y=1)
    by_y3, own_y3 = tie((from_zp, own_y3))
    other_y3 = move(by_y3, y=3)
    second_xp, from_xp = tie((second_xp, from_xp))
    by_z = pick(second_xp, from_xp)
    second_xp, second_zo, second_zp, by_z, shares = tie((second_xp, second_zo, second_zp, by_z, shares))

    third_xp = move(second_zo, x=1)
    third_xo = move_by_role(second_zo, native=(3, 0, 0, 0))
    third_z = move_by_role(by_z, native=(0, 0, 1, 0), far=(0, 0, 3, 0))
    third_z2 = move_by_role(second_xp, far=(0, 0, 2, 0))
    by_y1, other_y1 = tie((own_y3, other_y1))
    own_y2 = move(by_y1, y=1)
    by_y3, other_y3 = tie((other_y1, other_y3))
    other_y2 = move(by_y3, y=3)

    cutoff = threshold[0]
    residual, residual_other = shares[0].reshape(rows), shares[1].reshape(rows)
    weight = cutoff / jnp.maximum(jnp.abs(residual), cutoff)
    weight_other = cutoff / jnp.maximum(jnp.abs(residual_other), cutoff)
    influence = weight * residual
    local_grad = jnp.dot(influence, design.astype(jnp.float32), precision=lax.Precision.HIGHEST)
    spread_own = jnp.broadcast_to(weight[:, None], (rows, 128))
    spread = jnp.broadcast_to(weight_other[:, None], (rows, 128))
    blocks = row ^ jnp.arange(N_Y, dtype=jnp.int32)
    third_z, other_y1, other_y3 = tie((third_z, other_y1, other_y3))
    other_weighted = weigh(blocks, spread, [from_zp, other_y1, other_y3], (0, 1, 3))
    own_weighted = weigh(blocks, spread_own, [design, own_y1, own_y2, own_y3], (0, 1, 2, 3))
    column_a = pick(x, x ^ 3)
    column_b = column_a ^ 1
    own_slots = pick(jnp.array([0, 2, 7, 4]), jnp.array([0, 6, 1, 7]))
    other_slots = pick(jnp.array([1, 6, 3, 5]), jnp.array([3, 2, 5, 4]))

    def describe(core_at):
        places = ((column_a, zh), (column_a, 1 - zh), (column_b, zh), (column_b, 1 - zh))
        tiles = jnp.stack([column * 4 + at * 2 + core_at - 8 * slab for column, at in places])
        diagonal = tiles + 8 * slab == col
        return jnp.concatenate([tiles, diagonal, own_slots, other_slots, row[None], blocks[2:3]]).astype(jnp.int32)

    stack = jnp.stack([pick(design, from_xo), pick(from_zp, second_xp), second_zo, second_zp])
    third_z, own_weighted, other_weighted, spread, local_grad, stack, meta, meta_sibling = tie(
        (third_z, own_weighted, other_weighted, spread, local_grad, stack, describe(core), describe(1 - core)))
    gradient = -(local_grad + move(local_grad, z=1)) / samples
    here = [stack, third_xp, third_z, pick(from_zo, third_xo), pick(from_xp, third_z2)]
    *here, other_y2, gradient = tie((*here, other_y2, gradient))

    sibling = [move(shard, core=1) for shard in here]
    result, other_weighted = gram_blocks(
        meta, damping, own_weighted, other_weighted, here, samples, spread=spread, column=other_y2)
    result = gram_blocks(
        meta_sibling, damping, own_weighted, other_weighted, sibling, samples, into=result)
    hessian = result.reshape(2 * N_TILES, 1, width, N_Y * width)
    return (hessian, gradient)


def solution(mesh):
    in_specs = (P("slab", ("tcol", "trow")), P("slab"), P(("tcol", "trow")), P(), P())
    out_specs = (P("slab", "trow", None, "tcol"), P(("tcol", "trow")))
    return jax.shard_map(local, mesh=mesh, in_specs=in_specs, out_specs=out_specs, check_vma=False)
```

```python
import functools

import jax
import jax.numpy as jnp
from jax import lax
from jax.experimental import pallas as pl
from jax.experimental.pallas import tpu as pltpu
from jax.sharding import PartitionSpec as P

AXES = ("slab", "trow", "tcol")
N_X, N_Y, N_Z, N_CORE = 4, 4, 4, 2


def index_of(x, y, z, core):
    return ((z % 2) * N_Y + y) * 16 + x * 4 + (z // 2) * 2 + core


def is_native(x, z):
    return (x // 2) == (z % 2)


def pairs(route):
    found = []
    for x in range(N_X):
        for y in range(N_Y):
            for z in range(N_Z):
                step = route(x, z)
                if step is None:
                    continue
                dx, dy, dz, dcore = step
                for core in range(N_CORE):
                    target = index_of(x ^ dx, y ^ dy, z ^ dz, core ^ dcore)
                    found.append((index_of(x, y, z, core), target))
    return found


def move(value, x=0, y=0, z=0, core=0):
    return lax.ppermute(value, AXES, pairs(lambda cx, cz: (x, y, z, core)))


def move_by_role(value, native=None, far=None):
    return lax.ppermute(value, AXES, pairs(lambda cx, cz: native if is_native(cx, cz) else far))


def weigh_kernel(blocks_ref, spread_ref, *refs, places):
    *shard_refs, out_ref = refs
    lanes = spread_ref.shape[1]
    for m, shard_ref in zip(places, shard_refs):
        width = shard_ref.shape[1]
        for part in range(0, width, lanes):
            scaled = shard_ref[:, part:part + lanes].astype(jnp.float32) * spread_ref[...]
            at = pl.multiple_of(blocks_ref[m] * width + part, lanes)
            out_ref[:, pl.ds(at, lanes)] = scaled.astype(jnp.bfloat16)


def weigh(blocks, spread, shards, places):
    rows, width = shards[0].shape
    step = rows // 4

    def block(columns):
        return pl.BlockSpec((step, columns), lambda i, blocks: (i, 0))

    return pl.pallas_call(
        functools.partial(weigh_kernel, places=places),
        out_shape=jax.ShapeDtypeStruct((rows, width * N_Y), jnp.bfloat16),
        grid_spec=pltpu.PrefetchScalarGridSpec(
            num_scalar_prefetch=1,
            grid=(rows // step,),
            in_specs=[block(spread.shape[1])] + [block(width)] * len(shards),
            out_specs=block(width * N_Y),
        ),
        compiler_params=pltpu.CompilerParams(vmem_limit_bytes=60 * 2**20),
        cost_estimate=pl.CostEstimate(flops=0, bytes_accessed=0, transcendentals=0),
        name="weigh",
    )(blocks, spread, *shards)


N_TILES = 8
TILE_AT, DIAGONAL_AT, OWN_AT, OTHER_AT, ROW_AT, BLOCK_AT = 0, 8, 16, 24, 32, 33
FIRST_NEEDS = (1, 3)
LATER_NEEDS = ((2, 6), (7, 5), (4,), (8, 9, 11), (10, 14), (15, 13), (12,))
N_SLOTS = 16
N_CHUNKS = 4
AHEAD = 8


def gram_kernel(meta_ref, damping_ref, own_hbm, other_hbm, *refs, samples):
    spreads_hbm, columns_hbm, shards_hbm = refs[:2], refs[2:4], refs[4:4 + N_SLOTS]
    out_ref, weighted, slots, weighted_sems, slot_sems, columns, spreads, column_sems = refs[4 + N_SLOTS:]
    step = pl.program_id(0)
    contract = (((0,), (0,)), ((), ()))
    scale = 1.0 / samples
    chunk = weighted.shape[1] // N_CHUNKS

    def slot_copy(n):
        return pltpu.make_async_copy(shards_hbm[n], slots.at[n], slot_sems.at[n])

    def product(n, at):
        return lax.dot_general(
            slots[meta_ref[at + step]], weighted[n], contract, preferred_element_type=jnp.float32)

    def rows_at(j):
        return pl.ds(j * chunk, chunk)

    def weighted_copy(n, j):
        source = (own_hbm, other_hbm)[n]
        return pltpu.make_async_copy(source.at[rows_at(j)], weighted.at[n, rows_at(j)], weighted_sems.at[n, j])

    def part(n, at, j):
        return lax.dot_general(
            slots[meta_ref[at], rows_at(j)], weighted[n, rows_at(j)], contract, preferred_element_type=jnp.float32)

    def column_copies(n):
        return [
            pltpu.make_async_copy(columns_hbm[n], columns.at[n], column_sems.at[n, 0]),
            pltpu.make_async_copy(spreads_hbm[n], spreads.at[n], column_sems.at[n, 1])]

    def scale_column(n, j):
        width, lanes = columns.shape[2], spreads.shape[2]
        weight = spreads[n, rows_at(j), :]
        for first in range(0, width, lanes):
            scaled = columns[n, rows_at(j), first:first + lanes].astype(jnp.float32) * weight
            at = pl.multiple_of(meta_ref[BLOCK_AT] * width + first, lanes)
            weighted[n, rows_at(j), pl.ds(at, lanes)] = scaled.astype(jnp.bfloat16)

    @pl.when(step == 0)
    def _():
        queue = [slot_copy(0)] + column_copies(0) + [weighted_copy(0, j) for j in range(N_CHUNKS)]
        queue += [slot_copy(n) for n in FIRST_NEEDS]
        queue += column_copies(1)
        queue += [weighted_copy(1, j) for j in range(N_CHUNKS)]
        later = [slot_copy(n) for needed in LATER_NEEDS for n in needed]
        todo = queue + later
        for copy in todo[:AHEAD]:
            copy.start()
        waited = 0

        def wait(count):
            nonlocal waited
            for n in range(waited, waited + count):
                todo[n].wait()
                if n + AHEAD < len(todo):
                    todo[n + AHEAD].start()
            waited += count

        wait(3)
        for j in range(N_CHUNKS):
            wait(1)
            scale_column(0, j)
            if j == 0:
                out_ref[0] = part(0, OWN_AT, j)
            else:
                out_ref[0] += part(0, OWN_AT, j)
        wait(len(FIRST_NEEDS) + 2)
        for j in range(N_CHUNKS):
            wait(1)
            scale_column(1, j)
            if j < N_CHUNKS - 1:
                out_ref[0] += part(1, OTHER_AT, j)
            else:
                out_ref[0] = (out_ref[0] + part(1, OTHER_AT, j)) * scale
        for copy in todo[waited + AHEAD:]:
            copy.start()

    for at, needed in enumerate(LATER_NEEDS):
        @pl.when(step == at + 1)
        def _(needed=needed):
            for n in needed:
                slot_copy(n).wait()

    @pl.when(step > 0)
    def _():
        out_ref[0] = (product(0, OWN_AT) + product(1, OTHER_AT)) * scale

    @pl.when(meta_ref[DIAGONAL_AT + step] == 1)
    def _():
        height = out_ref.shape[1]
        at = pl.multiple_of(meta_ref[ROW_AT] * height, height)
        eye = (lax.broadcasted_iota(jnp.int32, (height, height), 0)
               == lax.broadcasted_iota(jnp.int32, (height, height), 1))
        out_ref[0, :, pl.ds(at, height)] += jnp.where(eye, damping_ref[0], 0.0)


def gram_blocks(meta, damping, own, other, spreads, columns, shards, samples):
    rows, height = shards[0].shape
    width = own.shape[1]
    arrays = [meta, damping, own, other, *spreads, *columns, *shards]
    return pl.pallas_call(
        functools.partial(gram_kernel, samples=samples),
        out_shape=jax.ShapeDtypeStruct((N_TILES, height, width), jnp.float32),
        grid_spec=pltpu.PrefetchScalarGridSpec(
            num_scalar_prefetch=1,
            grid=(N_TILES,),
            in_specs=[pl.BlockSpec(memory_space=pltpu.SMEM)] + [pl.BlockSpec(memory_space=pl.ANY)] * (len(arrays) - 2),
            out_specs=pl.BlockSpec((1, height, width), lambda i, meta: (meta[i], 0, 0)),
            scratch_shapes=[
                pltpu.VMEM((2, rows, width), jnp.bfloat16),
                pltpu.VMEM((N_SLOTS, rows, height), jnp.bfloat16),
                pltpu.SemaphoreType.DMA((2, N_CHUNKS)),
                pltpu.SemaphoreType.DMA((N_SLOTS,)),
                pltpu.VMEM((2, rows, height), jnp.bfloat16),
                pltpu.VMEM((2,) + spreads[0].shape, jnp.float32),
                pltpu.SemaphoreType.DMA((2, 2)),
            ],
        ),
        compiler_params=pltpu.CompilerParams(vmem_limit_bytes=60 * 2**20),
        cost_estimate=pl.CostEstimate(
            flops=N_TILES * 4 * rows * height * width, bytes_accessed=N_SLOTS * rows * height * 2, transcendentals=0),
        name="gram",
    )(*arrays)


def local(design, targets, coeffs, threshold, damping):
    rows, width = design.shape
    samples = rows * lax.axis_size("slab")
    slab, row, col = lax.axis_index("slab"), lax.axis_index("trow"), lax.axis_index("tcol")
    x, zh, core = col // 4, (col // 2) % 2, col % 2
    native = (x // 2) == slab
    tie = lax.optimization_barrier

    def pick(if_native, if_far):
        return jnp.where(native, if_native, if_far)

    first = (row == 0) & (col == 0)
    share = jnp.where(first, targets, 0.0) - jnp.dot(design, coeffs, preferred_element_type=jnp.float32)
    share = share.reshape(rows // 128, 128)
    share = share + move(share, z=2)
    design_z, share = tie((design, share))
    from_zp = move(design_z, z=1)
    from_zo = move(design_z, z=3)
    share = (share + move(share, x=1)) + (move(share, x=3) + move(share, x=2))
    design_x, share = tie((design, share))
    from_xo = move(design_x, x=3)
    from_xp = move(design_x, x=1)
    for where in ({"core": 1}, {"y": 1}, {"y": 2}):
        share = share + move(share, **where)
    design_y, share = tie((design, share))
    own_y1 = move(design_y, y=1)
    own_y3 = move(design_y, y=3)
    from_zp, from_zo, from_xp, from_xo, share = tie((from_zp, from_zo, from_xp, from_xo, share))

    second_xp = move(from_xo, x=1)
    by_zo, by_zp, shares = tie(
        (pick(from_xo, from_zp), pick(from_xo, from_xp), jnp.stack([share, move(share, z=1)])))
    second_zo = move(by_zo, z=3)
    second_zp = move(by_zp, z=1)
    by_y1, own_y1 = tie((from_zp, own_y1))
    other_y1 = move(by_y1, y=1)
    by_y3, own_y3 = tie((from_zp, own_y3))
    other_y3 = move(by_y3, y=3)
    second_xp, from_xp = tie((second_xp, from_xp))
    by_z = pick(second_xp, from_xp)
    second_xp, second_zo, second_zp, by_z, shares = tie((second_xp, second_zo, second_zp, by_z, shares))

    third_xp = move(second_zo, x=1)
    third_xo = move_by_role(second_zo, native=(3, 0, 0, 0))
    third_z = move_by_role(by_z, native=(0, 0, 1, 0), far=(0, 0, 3, 0))
    third_z2 = move_by_role(second_xp, far=(0, 0, 2, 0))
    by_y1, other_y1 = tie((own_y3, other_y1))
    own_y2 = move(by_y1, y=1)
    by_y3, other_y3 = tie((other_y1, other_y3))
    other_y2 = move(by_y3, y=3)

    cutoff = threshold[0]
    residual, residual_other = shares[0].reshape(rows), shares[1].reshape(rows)
    weight = cutoff / jnp.maximum(jnp.abs(residual), cutoff)
    weight_other = cutoff / jnp.maximum(jnp.abs(residual_other), cutoff)
    influence = weight * residual
    local_grad = jnp.dot(influence, design.astype(jnp.float32), precision=lax.Precision.HIGHEST)
    spread_own = jnp.broadcast_to(weight[:, None], (rows, 128))
    spread = jnp.broadcast_to(weight_other[:, None], (rows, 128))
    blocks = row ^ jnp.arange(N_Y, dtype=jnp.int32)
    third_xp, third_xo, other_y1, other_y3 = tie((third_xp, third_xo, other_y1, other_y3))
    other_weighted = weigh(blocks, spread, [from_zp, other_y1, other_y3], (0, 1, 3))
    own_weighted = weigh(blocks, spread_own, [design, own_y1, own_y3], (0, 1, 3))
    column_a = pick(x, x ^ 3)
    column_b = column_a ^ 1
    own_slots = pick(jnp.array([0, 2, 7, 4, 8, 10, 15, 12]), jnp.array([0, 6, 1, 7, 8, 14, 9, 15]))
    other_slots = pick(jnp.array([1, 6, 3, 5, 9, 14, 11, 13]), jnp.array([3, 2, 5, 4, 11, 10, 13, 12]))
    places = ((column_a, zh), (column_a, 1 - zh), (column_b, zh), (column_b, 1 - zh))
    tiles = jnp.stack([column * 4 + at * 2 + core_at - 8 * slab for core_at in (core, 1 - core) for column, at in places])
    diagonal = tiles + 8 * slab == col
    meta = jnp.concatenate([tiles, diagonal, own_slots, other_slots, row[None], blocks[2:3]]).astype(jnp.int32)

    early = [pick(design, from_xo), pick(from_zp, second_xp), second_zo, second_zp]
    third_xp, third_z, third_xo, own_weighted, other_weighted, spread_own, spread, local_grad, meta, *early = tie(
        (third_xp, third_z, third_xo, own_weighted, other_weighted, spread_own, spread, local_grad, meta, *early))
    gradient = -(local_grad + move(local_grad, z=1)) / samples
    here = [*early, third_xp, third_z, pick(from_zo, third_xo), pick(from_xp, third_z2)]
    sibling = [move(shard, core=1) for shard in here]
    result = gram_blocks(
        meta, damping, own_weighted, other_weighted, (spread_own, spread), (own_y2, other_y2), here + sibling, samples)
    hessian = result.reshape(N_TILES, 1, width, N_Y * width)
    return (hessian, gradient)


def solution(mesh):
    in_specs = (P("slab", ("tcol", "trow")), P("slab"), P(("tcol", "trow")), P(), P())
    out_specs = (P("slab", "trow", None, "tcol"), P(("tcol", "trow")))
    return jax.shard_map(local, mesh=mesh, in_specs=in_specs, out_specs=out_specs, check_vma=False)
```

```python
import functools

import jax
import jax.numpy as jnp
from jax import lax
from jax.experimental import pallas as pl
from jax.experimental.pallas import tpu as pltpu
from jax.sharding import PartitionSpec as P

AXES = ("slab", "trow", "tcol")
N_X, N_Y, N_Z, N_CORE = 4, 4, 4, 2


def index_of(x, y, z, core):
    return ((z % 2) * N_Y + y) * 16 + x * 4 + (z // 2) * 2 + core


def is_native(x, z):
    return (x // 2) == (z % 2)


def pairs(route):
    found = []
    for x in range(N_X):
        for y in range(N_Y):
            for z in range(N_Z):
                step = route(x, z)
                if step is None:
                    continue
                dx, dy, dz, dcore = step
                for core in range(N_CORE):
                    target = index_of(x ^ dx, y ^ dy, z ^ dz, core ^ dcore)
                    found.append((index_of(x, y, z, core), target))
    return found


def move(value, x=0, y=0, z=0, core=0):
    return lax.ppermute(value, AXES, pairs(lambda cx, cz: (x, y, z, core)))


def move_by_role(value, native=None, far=None):
    return lax.ppermute(value, AXES, pairs(lambda cx, cz: native if is_native(cx, cz) else far))


def weigh_kernel(blocks_ref, spread_ref, *refs, places):
    *shard_refs, out_ref = refs
    lanes = spread_ref.shape[1]
    for m, shard_ref in zip(places, shard_refs):
        width = shard_ref.shape[1]
        for part in range(0, width, lanes):
            scaled = shard_ref[:, part:part + lanes].astype(jnp.float32) * spread_ref[...]
            at = pl.multiple_of(blocks_ref[m] * width + part, lanes)
            out_ref[:, pl.ds(at, lanes)] = scaled.astype(jnp.bfloat16)


def weigh(blocks, spread, shards, places):
    rows, width = shards[0].shape
    step = rows // 4

    def block(columns):
        return pl.BlockSpec((step, columns), lambda i, blocks: (i, 0))

    return pl.pallas_call(
        functools.partial(weigh_kernel, places=places),
        out_shape=jax.ShapeDtypeStruct((rows, width * N_Y), jnp.bfloat16),
        grid_spec=pltpu.PrefetchScalarGridSpec(
            num_scalar_prefetch=1,
            grid=(rows // step,),
            in_specs=[block(spread.shape[1])] + [block(width)] * len(shards),
            out_specs=block(width * N_Y),
        ),
        compiler_params=pltpu.CompilerParams(vmem_limit_bytes=60 * 2**20),
        cost_estimate=pl.CostEstimate(flops=0, bytes_accessed=0, transcendentals=0),
        name="weigh",
    )(blocks, spread, *shards)


N_TILES = 8
TILE_AT, DIAGONAL_AT, OWN_AT, OTHER_AT, ROW_AT, BLOCK_AT = 0, 8, 16, 24, 32, 33
FIRST_NEEDS = (1, 3)
LATER_NEEDS = ((2, 6), (7, 5), (4,), (8, 9, 11), (10, 14), (15, 13), (12,))
N_SLOTS = 16
N_CHUNKS = 4
AHEAD = 8


def gram_kernel(meta_ref, damping_ref, own_hbm, other_hbm, *refs, samples):
    spreads_hbm, columns_hbm = refs[:2], refs[2:4]
    shards_hbm = []
    for early, *others in (refs[4:11], refs[11:18]):
        shards_hbm += [early.at[0], early.at[1], *others]
    out_ref, weighted, slots, weighted_sems, slot_sems, columns, spreads, column_sems = refs[18:]
    step = pl.program_id(0)
    contract = (((0,), (0,)), ((), ()))
    scale = 1.0 / samples
    chunk = weighted.shape[1] // N_CHUNKS

    def slot_copy(n):
        return pltpu.make_async_copy(shards_hbm[n], slots.at[n], slot_sems.at[n])

    def product(n, at):
        return lax.dot_general(
            slots[meta_ref[at + step]], weighted[n], contract, preferred_element_type=jnp.float32)

    def rows_at(j):
        return pl.ds(j * chunk, chunk)

    def weighted_copy(n, j):
        source = (own_hbm, other_hbm)[n]
        return pltpu.make_async_copy(source.at[rows_at(j)], weighted.at[n, rows_at(j)], weighted_sems.at[n, j])

    def part(n, at, j):
        return lax.dot_general(
            slots[meta_ref[at], rows_at(j)], weighted[n, rows_at(j)], contract, preferred_element_type=jnp.float32)

    def column_copies(n):
        return [
            pltpu.make_async_copy(columns_hbm[n], columns.at[n], column_sems.at[n, 0]),
            pltpu.make_async_copy(spreads_hbm[n], spreads.at[n], column_sems.at[n, 1])]

    def scale_column(n, j):
        width, lanes = columns.shape[2], spreads.shape[2]
        weight = spreads[n, rows_at(j), :]
        for first in range(0, width, lanes):
            scaled = columns[n, rows_at(j), first:first + lanes].astype(jnp.float32) * weight
            at = pl.multiple_of(meta_ref[BLOCK_AT] * width + first, lanes)
            weighted[n, rows_at(j), pl.ds(at, lanes)] = scaled.astype(jnp.bfloat16)

    @pl.when(step == 0)
    def _():
        queue = [slot_copy(0)] + column_copies(0) + [weighted_copy(0, j) for j in range(N_CHUNKS)]
        queue += [slot_copy(n) for n in FIRST_NEEDS]
        queue += column_copies(1)
        queue += [weighted_copy(1, j) for j in range(N_CHUNKS)]
        later = [slot_copy(n) for needed in LATER_NEEDS for n in needed]
        todo = queue + later
        for copy in todo[:AHEAD]:
            copy.start()
        waited = 0

        def wait(count):
            nonlocal waited
            for n in range(waited, waited + count):
                todo[n].wait()
                if n + AHEAD < len(todo):
                    todo[n + AHEAD].start()
            waited += count

        wait(3)
        for j in range(N_CHUNKS):
            wait(1)
            scale_column(0, j)
            if j == 0:
                out_ref[0] = part(0, OWN_AT, j)
            else:
                out_ref[0] += part(0, OWN_AT, j)
        wait(len(FIRST_NEEDS) + 2)
        for j in range(N_CHUNKS):
            wait(1)
            scale_column(1, j)
            if j < N_CHUNKS - 1:
                out_ref[0] += part(1, OTHER_AT, j)
            else:
                out_ref[0] = (out_ref[0] + part(1, OTHER_AT, j)) * scale
        for copy in todo[waited + AHEAD:]:
            copy.start()

    for at, needed in enumerate(LATER_NEEDS):
        @pl.when(step == at + 1)
        def _(needed=needed):
            for n in needed:
                slot_copy(n).wait()

    @pl.when(step > 0)
    def _():
        out_ref[0] = (product(0, OWN_AT) + product(1, OTHER_AT)) * scale

    @pl.when(meta_ref[DIAGONAL_AT + step] == 1)
    def _():
        height = out_ref.shape[1]
        at = pl.multiple_of(meta_ref[ROW_AT] * height, height)
        eye = (lax.broadcasted_iota(jnp.int32, (height, height), 0)
               == lax.broadcasted_iota(jnp.int32, (height, height), 1))
        out_ref[0, :, pl.ds(at, height)] += jnp.where(eye, damping_ref[0], 0.0)


def gram_blocks(meta, damping, own, other, spreads, columns, shards, samples):
    rows, height = shards[1].shape
    width = own.shape[1]
    arrays = [meta, damping, own, other, *spreads, *columns, *shards]
    return pl.pallas_call(
        functools.partial(gram_kernel, samples=samples),
        out_shape=jax.ShapeDtypeStruct((N_TILES, height, width), jnp.float32),
        grid_spec=pltpu.PrefetchScalarGridSpec(
            num_scalar_prefetch=1,
            grid=(N_TILES,),
            in_specs=[pl.BlockSpec(memory_space=pltpu.SMEM)] + [pl.BlockSpec(memory_space=pl.ANY)] * (len(arrays) - 2),
            out_specs=pl.BlockSpec((1, height, width), lambda i, meta: (meta[i], 0, 0)),
            scratch_shapes=[
                pltpu.VMEM((2, rows, width), jnp.bfloat16),
                pltpu.VMEM((N_SLOTS, rows, height), jnp.bfloat16),
                pltpu.SemaphoreType.DMA((2, N_CHUNKS)),
                pltpu.SemaphoreType.DMA((N_SLOTS,)),
                pltpu.VMEM((2, rows, height), jnp.bfloat16),
                pltpu.VMEM((2,) + spreads[0].shape, jnp.float32),
                pltpu.SemaphoreType.DMA((2, 2)),
            ],
        ),
        compiler_params=pltpu.CompilerParams(vmem_limit_bytes=60 * 2**20),
        cost_estimate=pl.CostEstimate(
            flops=N_TILES * 4 * rows * height * width, bytes_accessed=N_SLOTS * rows * height * 2, transcendentals=0),
        name="gram",
    )(*arrays)


def local(design, targets, coeffs, threshold, damping):
    rows, width = design.shape
    samples = rows * lax.axis_size("slab")
    slab, row, col = lax.axis_index("slab"), lax.axis_index("trow"), lax.axis_index("tcol")
    x, zh, core = col // 4, (col // 2) % 2, col % 2
    native = (x // 2) == slab
    tie = lax.optimization_barrier

    def pick(if_native, if_far):
        return jnp.where(native, if_native, if_far)

    first = (row == 0) & (col == 0)
    share = jnp.where(first, targets, 0.0) - jnp.dot(design, coeffs, preferred_element_type=jnp.float32)
    share = share.reshape(rows // 128, 128)
    share = share + move(share, z=2)
    design_z, share = tie((design, share))
    from_zp = move(design_z, z=1)
    from_zo = move(design_z, z=3)
    share = (share + move(share, x=1)) + (move(share, x=3) + move(share, x=2))
    design_x, share = tie((design, share))
    from_xo = move(design_x, x=3)
    from_xp = move(design_x, x=1)
    for where in ({"core": 1}, {"y": 1}, {"y": 2}):
        share = share + move(share, **where)
    design_y, share = tie((design, share))
    own_y1 = move(design_y, y=1)
    own_y3 = move(design_y, y=3)
    from_zp, from_zo, from_xp, from_xo, share = tie((from_zp, from_zo, from_xp, from_xo, share))

    second_xp = move(from_xo, x=1)
    by_zo, by_zp, shares = tie(
        (pick(from_xo, from_zp), pick(from_xo, from_xp), jnp.stack([share, move(share, z=1)])))
    second_zo = move(by_zo, z=3)
    second_zp = move(by_zp, z=1)
    by_y1, own_y1 = tie((from_zp, own_y1))
    other_y1 = move(by_y1, y=1)
    by_y3, own_y3 = tie((from_zp, own_y3))
    other_y3 = move(by_y3, y=3)
    second_xp, from_xp = tie((second_xp, from_xp))
    by_z = pick(second_xp, from_xp)
    second_xp, second_zo, second_zp, by_z, shares = tie((second_xp, second_zo, second_zp, by_z, shares))

    third_xp = move(second_zo, x=1)
    third_xo = move_by_role(second_zo, native=(3, 0, 0, 0))
    third_z = move_by_role(by_z, native=(0, 0, 1, 0), far=(0, 0, 3, 0))
    third_z2 = move_by_role(second_xp, far=(0, 0, 2, 0))
    by_y1, other_y1 = tie((own_y3, other_y1))
    own_y2 = move(by_y1, y=1)
    by_y3, other_y3 = tie((other_y1, other_y3))
    other_y2 = move(by_y3, y=3)

    cutoff = threshold[0]
    residual, residual_other = shares[0].reshape(rows), shares[1].reshape(rows)
    weight = cutoff / jnp.maximum(jnp.abs(residual), cutoff)
    weight_other = cutoff / jnp.maximum(jnp.abs(residual_other), cutoff)
    influence = weight * residual
    local_grad = jnp.dot(influence, design.astype(jnp.float32), precision=lax.Precision.HIGHEST)
    spread_own = jnp.broadcast_to(weight[:, None], (rows, 128))
    spread = jnp.broadcast_to(weight_other[:, None], (rows, 128))
    blocks = row ^ jnp.arange(N_Y, dtype=jnp.int32)
    third_xp, third_xo, other_y1, other_y3 = tie((third_xp, third_xo, other_y1, other_y3))
    other_weighted = weigh(blocks, spread, [from_zp, other_y1, other_y3], (0, 1, 3))
    own_weighted = weigh(blocks, spread_own, [design, own_y1, own_y3], (0, 1, 3))
    column_a = pick(x, x ^ 3)
    column_b = column_a ^ 1
    own_slots = pick(jnp.array([0, 2, 7, 4, 8, 10, 15, 12]), jnp.array([0, 6, 1, 7, 8, 14, 9, 15]))
    other_slots = pick(jnp.array([1, 6, 3, 5, 9, 14, 11, 13]), jnp.array([3, 2, 5, 4, 11, 10, 13, 12]))
    places = ((column_a, zh), (column_a, 1 - zh), (column_b, zh), (column_b, 1 - zh))
    tiles = jnp.stack([column * 4 + at * 2 + core_at - 8 * slab for core_at in (core, 1 - core) for column, at in places])
    diagonal = tiles + 8 * slab == col
    meta = jnp.concatenate([tiles, diagonal, own_slots, other_slots, row[None], blocks[2:3]]).astype(jnp.int32)

    early = [jnp.stack([pick(design, from_xo), pick(from_zp, second_xp)]), second_zo, second_zp]
    third_xp, third_z, third_xo, own_weighted, other_weighted, spread_own, spread, local_grad, meta, *early = tie(
        (third_xp, third_z, third_xo, own_weighted, other_weighted, spread_own, spread, local_grad, meta, *early))
    here = [*early, third_xp, third_z, pick(from_zo, third_xo), pick(from_xp, third_z2)]
    sibling = [move(shard, core=1) for shard in here]
    sibling[-1], local_grad = tie((sibling[-1], local_grad))
    gradient = -(local_grad + move(local_grad, z=1)) / samples
    result = gram_blocks(
        meta, damping, own_weighted, other_weighted, (spread_own, spread), (own_y2, other_y2), here + sibling, samples)
    hessian = result.reshape(N_TILES, 1, width, N_Y * width)
    return (hessian, gradient)


def solution(mesh):
    in_specs = (P("slab", ("tcol", "trow")), P("slab"), P(("tcol", "trow")), P(), P())
    out_specs = (P("slab", "trow", None, "tcol"), P(("tcol", "trow")))
    return jax.shard_map(local, mesh=mesh, in_specs=in_specs, out_specs=out_specs, check_vma=False)
```
